256 devices in a mesh: dom: 256 (over z, y, x, core).
Axes of the slice: x: 4, y: 4, z: 8, core: 2. Of those that a mesh axis runs over, the one named last changes fastest.
Arguments:
- features: bfloat16 [64, 2097152], P(None, 'dom'), may hold values from -6 to 6
- cheb_weight: bfloat16 [4, 64, 64], replicated, may hold values from -0.375 to 0.375
- lap_tiles: bfloat16 [16384, 3, 128, 128], P('dom'), may hold values from -0.25 to 0.25
- col_index: int32 [16384, 3], P('dom'), may hold values from 0 to 63
- cross_tiles: bfloat16 [256, 5, 2, 128, 128], P('dom'), may hold values from -0.25 to 0.25
- send_index: int32 [256, 5, 2], P('dom'), may hold values from 0 to 63
- row_index: int32 [256, 5, 2], P('dom'), may hold values from 0 to 63
- pair_on: int32 [256, 5], P('dom'), may hold values 0 or 1
- blk_live: int32 [256], P('dom'), may hold values from 1 to 64, 12288 in all
- cotangent: bfloat16 [64, 2097152], P(None, 'dom'), may hold values from -6 to 6
Outputs:
- conv_out: bfloat16 [64, 2097152], P(None, 'dom')
- grad_x: bfloat16 [64, 2097152], P(None, 'dom')
- grad_w: float32 [4, 64, 64], replicated
The draws below stay inside these ranges and needn't reach their ends.
Inputs may be any that keep to these rules, and one draw needn't show every extreme that they name: `blk_live`: the counts sum to 12288 and the largest is exactly 64.
All inputs are finite; a program needn't handle non-finite values. No bound on the sum of `pair_on` or of `blk_live` on one device may be relied on, other than what follows from the above.
Results may differ from the reference program's by a relative error of at most 0.0059.
Values may be sent and summed in bfloat16 or wider, within the bound.
A program may use at most 128 MiB of HBM per device.

```python
import math
import jax
import jax.numpy as jnp
import numpy as np
from jax import lax

F = 64
ORDER = 3
BLK = 128
NB = 64
NZ = 3
HB = 2
ROUNDS = 5
NBLOCKS = 16384
PIXELS = 2097152
N_DOM = 256


def touch_ends(result, own_key, low, largest):
    longest = result.shape.index(max(result.shape))
    spots = []
    for shift in (0, 1):
        where = [jax.random.randint(jax.random.fold_in(own_key, axis), (), 0, length) for axis, length in enumerate(result.shape)]
        where[longest] = (where[longest] + shift) % result.shape[longest]
        spots.append(tuple(where))
    return result.at[spots[0]].set(low).at[spots[1]].set(largest)


def steps_of(rng, shape, shards, low, largest):
    factor_of, own = 1.0, jax.random.fold_in(rng, 6)
    for axis_at, blocks in shards:
        heights = jnp.exp(jax.random.uniform(jax.random.fold_in(own, axis_at), (blocks,), jnp.float32, low / len(shards), largest / len(shards)))
        factor_of = factor_of * jnp.repeat(heights, shape[axis_at] // blocks).reshape([-1 if axis == axis_at else 1 for axis in range(len(shape))])
    return factor_of


def profile(number_of, total, limit, slope):
    weights = [(1 << 20) // math.isqrt(rank ** slope) + 1 for rank in range(2, number_of + 1)]
    rest, counts = total - limit - (number_of - 1), [1] * (number_of - 1)
    while rest > 0:
        movable = [i for i in range(number_of - 1) if counts[i] < limit]
        mass, budget = sum([weights[i] for i in movable]), rest
        for i in movable:
            extra = min(limit - counts[i], max(1, budget * weights[i] // mass), rest)
            counts[i] = counts[i] + extra
            rest = rest - extra
    return np.array([limit] + counts)


def uneven_parts(key, number_of, total, reach, slope):
    if number_of == 2:
        one = jax.random.randint(key, (), max(1, total - reach), min(reach, total - 1) + 1)
        return jnp.stack([one, total - one])
    tallies = jnp.asarray(profile(number_of, total, reach, slope), jnp.int32)
    twos = (number_of - 1) // 2
    giver, sink = tallies[1:1 + 2 * twos:2], tallies[2:2 + 2 * twos:2]
    margin = jnp.minimum(giver - 1, reach - sink)
    shifted = jax.random.randint(jax.random.fold_in(key, 1), (twos,), 0, 1 << 20) % (margin + 1)
    tallies = tallies.at[1:1 + 2 * twos:2].set(giver - shifted).at[2:2 + 2 * twos:2].set(sink + shifted)
    return tallies[jax.random.permutation(jax.random.fold_in(key, 2), number_of)]


def gaussian(stream_key, shape, width, most, shards=(), kind=jnp.bfloat16):
    result = jax.random.normal(stream_key, shape, jnp.float32) * width
    if len(shards) > 0:
        result = steps_of(stream_key, shape, shards, -0.22, 0.18) * result
    return jnp.clip(result, min=-most, max=most).astype(kind)


def setup_inputs(seed: int = 0) -> dict:
    streams_of = jax.random.split(jax.random.key(seed), 11)
    features = gaussian(streams_of[0], (F, PIXELS), 1.0, 6.0, ((1, 256),))
    cheb_weight = gaussian(streams_of[1], (ORDER + 1, F, F), (F * (ORDER + 1)) ** -0.5, 0.375)
    lap_tiles = gaussian(streams_of[2], (NBLOCKS, NZ, BLK, BLK), (BLK * (NZ + 1)) ** -0.5, 0.25, ((0, 256),))
    col_index = touch_ends(jax.random.randint(streams_of[3], (NBLOCKS, NZ), 0, NB), jax.random.fold_in(streams_of[3], 1), 0, NB - 1).astype(jnp.int32)
    cross_tiles = gaussian(streams_of[4], (N_DOM, ROUNDS, HB, BLK, BLK), (BLK * (NZ + 1)) ** -0.5, 0.25, ((0, 256),))
    send_index = touch_ends(jax.random.randint(streams_of[5], (N_DOM, ROUNDS, HB), 0, NB), jax.random.fold_in(streams_of[5], 1), 0, NB - 1).astype(jnp.int32)
    row_index = touch_ends(jax.random.randint(streams_of[6], (N_DOM, ROUNDS, HB), 0, NB), jax.random.fold_in(streams_of[6], 1), 0, NB - 1).astype(jnp.int32)
    pair_on = touch_ends((jax.random.randint(streams_of[7], (N_DOM, ROUNDS), 0, 4) < 3).astype(jnp.int32), jax.random.fold_in(streams_of[7], 1), 0, 1)
    blk_live = uneven_parts(streams_of[8], N_DOM, (3 * NB * N_DOM) // 4, NB, 2).astype(jnp.int32)
    cotangent = gaussian(streams_of[9], (F, PIXELS), 1.0, 6.0, ((1, 256),))
    return dict(features=features, cheb_weight=cheb_weight, lap_tiles=lap_tiles, col_index=col_index, cross_tiles=cross_tiles, send_index=send_index, row_index=row_index, pair_on=pair_on, blk_live=blk_live, cotangent=cotangent)


def to_blocks(values):
    return values.reshape(values.shape[0], N_DOM, NB, BLK).transpose(1, 0, 2, 3)


def from_blocks(values):
    return values.transpose(1, 0, 2, 3).reshape(values.shape[1], N_DOM * NB * BLK)


def reference(features, cheb_weight, lap_tiles, col_index, cross_tiles, send_index, row_index, pair_on, blk_live, cotangent):
    highest = lax.Precision.HIGHEST
    tiles = lap_tiles.reshape(N_DOM, NB, NZ, BLK, BLK)
    columns = col_index.reshape(N_DOM, NB, NZ)
    owners = jnp.arange(N_DOM, dtype=jnp.int32)
    live_blocks = blk_live.astype(jnp.int32)
    mask_full = (jnp.arange(NB, dtype=jnp.int32)[None, :] < live_blocks[:, None]).astype(jnp.float32)[:, None, :, None]
    mask_half = mask_full.astype(jnp.bfloat16)
    send_rows = (send_index % live_blocks[:, None, None]).astype(jnp.int32)
    recv_rows = (row_index % live_blocks[:, None, None]).astype(jnp.int32)
    switch = pair_on.astype(jnp.float32)
    coupling = cross_tiles.astype(jnp.float32)
    weights = cheb_weight.astype(jnp.float32)

    take_rows = jax.vmap(lambda values, rows: jnp.take(values, rows, axis=1))
    add_rows = jax.vmap(lambda summed, rows, terms: summed.at[:, rows].add(terms))

    def local_forward(args):
        part_tiles, part_cols, part_values = args
        gathered = jnp.take(part_values, part_cols, axis=1).astype(jnp.float32)
        return jnp.einsum("inab,finb->fia", part_tiles.astype(jnp.float32), gathered, precision=highest)

    def local_adjoint(args):
        part_tiles, part_cols, part_values = args
        terms = jnp.einsum("inab,fia->finb", part_tiles.astype(jnp.float32), part_values.astype(jnp.float32), precision=highest)
        return jnp.zeros((F, NB, BLK), jnp.float32).at[:, part_cols].add(terms)

    def apply_forward(values):
        summed = lax.map(local_forward, (tiles, columns, values))
        for level in range(ROUNDS):
            partner = jnp.bitwise_xor(owners, 1 << level).astype(jnp.int32)
            incoming = take_rows(values, send_rows[:, level])[partner].astype(jnp.float32)
            product = jnp.einsum("nhab,nfhb->nfha", coupling[:, level], incoming, precision=highest)
            product = product * switch[:, level][:, None, None, None]
            summed = add_rows(summed, recv_rows[:, level], product)
        return summed

    def apply_adjoint(values):
        summed = lax.map(local_adjoint, (tiles, columns, values))
        for level in range(ROUNDS):
            partner = jnp.bitwise_xor(owners, 1 << level).astype(jnp.int32)
            pieces = take_rows(values, recv_rows[:, level]).astype(jnp.float32)
            terms = jnp.einsum("nhab,nfha->nfhb", coupling[:, level], pieces, precision=highest)
            terms = terms * switch[:, level][:, None, None, None]
            summed = add_rows(summed, send_rows[:, level], terms[partner])
        return summed

    zeroth = to_blocks(features) * mask_half
    first = (apply_forward(zeroth) * mask_full).astype(jnp.bfloat16)
    second = ((2.0 * apply_forward(first) - zeroth.astype(jnp.float32)) * mask_full).astype(jnp.bfloat16)
    third = ((2.0 * apply_forward(second) - first.astype(jnp.float32)) * mask_full).astype(jnp.bfloat16)
    orders = [zeroth, first, second, third]

    output = jnp.zeros((N_DOM, F, NB, BLK), jnp.float32)
    for level in range(ORDER + 1):
        output = output + jnp.einsum("fg,nfib->ngib", weights[level], orders[level].astype(jnp.float32), precision=highest)
    conv_out = from_blocks((output * mask_full).astype(jnp.bfloat16))

    upstream = (to_blocks(cotangent) * mask_half).astype(jnp.float32)
    grad_w = jnp.stack([jnp.einsum("nfib,ngib->fg", orders[level].astype(jnp.float32), upstream, precision=highest) for level in range(ORDER + 1)])
    lifted = [jnp.einsum("fg,ngib->nfib", weights[level], upstream, precision=highest) for level in range(ORDER + 1)]

    back_third = (lifted[3] * mask_full).astype(jnp.bfloat16)
    adjoint_two = lifted[2] + 2.0 * apply_adjoint(back_third)
    back_second = (adjoint_two * mask_full).astype(jnp.bfloat16)
    adjoint_one = lifted[1] + 2.0 * apply_adjoint(back_second) - back_third.astype(jnp.float32)
    back_first = (adjoint_one * mask_full).astype(jnp.bfloat16)
    adjoint_zero = lifted[0] + apply_adjoint(back_first) - back_second.astype(jnp.float32)
    grad_x = from_blocks((adjoint_zero * mask_full).astype(jnp.bfloat16))
    return (conv_out, grad_x, grad_w)
```

```python
import functools

import jax
import jax.numpy as jnp
from jax import lax
from jax.experimental import pallas as pl
from jax.experimental.pallas import tpu as pltpu
from jax.sharding import PartitionSpec as P

F32 = jnp.float32
BF16 = jnp.bfloat16
I32 = jnp.int32
MESH = pl.DeviceIdType.MESH
GROUP = 16
CHUNKS = 8


def dot(a, b):
    return jnp.dot(a, b, preferred_element_type=F32)


def small_mod(value, count, largest):
    power = 1
    while power * 2 <= largest:
        power *= 2
    while power >= 1:
        step = count * power
        value = jnp.where(value >= step, value - step, value)
        power //= 2
    return value


def kernel(
    size,
    feat_hbm, cheb_ref, lap_hbm, col_vmem, col, cross_hbm, send_ref, row_ref, pair_ref, live_ref, cot_hbm,
    conv_hbm, gradx_hbm, gradw_ref,
    feat, cot, lap, lap_t, cross, cross_t, field, back, up, up_t, chain0, chain1, chain2, coup,
    send_f, recv_f, send_b, recv_b, conv, gradx, idx_v, idx, sends, rows, part, got1, mine2, got2, mine3, got3,
    load_sem, lap_sem, idx_sem, out_sem, sf_sem, rf_sem, sb_sem, rb_sem,
    s1_sem, r1_sem, s2_sem, r2_sem, s3_sem, r3_sem,
):
    blocks, width, block = lap.shape[0], feat.shape[0], lap.shape[2]
    nz = lap.shape[1]
    rounds = 5
    coups = 2 * rounds
    chains = (chain0, chain1, chain2)
    me = lax.axis_index("dom")
    near, far = me % GROUP, me // GROUP
    far_size = size // GROUP

    def partner(level):
        bit = (me // (1 << level)) % 2
        return me + (1 << level) * (1 - 2 * bit)

    def near_peer(step):
        return far * GROUP + (near + step) % GROUP

    def far_peer(step):
        return ((far + step) % far_size) * GROUP + near

    per = blocks // CHUNKS
    loads = [
        pltpu.make_async_copy(feat_hbm, feat, load_sem.at[0]),
        pltpu.make_async_copy(cot_hbm, cot, load_sem.at[1]),
        pltpu.make_async_copy(cross_hbm, cross, load_sem.at[2]),
    ]
    for load in loads:
        load.start()

    def lap_load(part_at):
        where = pl.ds(part_at * per, per)
        return pltpu.make_async_copy(lap_hbm.at[where], lap.at[where], lap_sem.at[part_at])

    for part_at in range(CHUNKS):
        lap_load(part_at).start()

    barrier = pltpu.get_barrier_semaphore()
    for level in range(rounds):
        pl.semaphore_signal(barrier, inc=1, device_id=(partner(level),), device_id_type=MESH)

    @pl.loop(1, GROUP)
    def _(step):
        pl.semaphore_signal(barrier, inc=1, device_id=(near_peer(step),), device_id_type=MESH)

    if far_size > 1:
        @pl.loop(1, far_size)
        def _(step):
            pl.semaphore_signal(barrier, inc=1, device_id=(far_peer(step),), device_id_type=MESH)

    live = live_ref[0]

    def mask_of(i):
        return (i < live).astype(F32)

    for k in range(coups):
        sends[0, k] = small_mod(send_ref[0, k // 2, k % 2], live, blocks - 1)
        rows[0, k] = small_mod(row_ref[0, k // 2, k % 2], live, blocks - 1)
    for table in (sends, rows):
        for k in range(coups):
            before = jnp.int32(coups)
            for other in range(k):
                before = jnp.where(table[0, other] == table[0, k], other, before)
            table[1, k] = before
    at_sub = lax.broadcasted_iota(I32, (blocks, 128), 0)
    at_lane = lax.broadcasted_iota(I32, (blocks, 128), 1)
    lane = lax.broadcasted_iota(I32, (1, 128), 1)
    for n in range(nz):
        cols = jnp.broadcast_to(col_vmem[:, n : n + 1], (blocks, 128))
        turned = jnp.sum(jnp.where(at_sub == at_lane, cols, 0), axis=0, keepdims=True)
        same = (cols == turned) & (at_sub < at_lane)
        prev = jnp.max(jnp.where(same, at_sub, -1), axis=0, keepdims=True)
        last = jnp.max(jnp.where(cols == at_lane, at_sub, -1), axis=0, keepdims=True)
        idx_v[n : n + 1, :] = jnp.where(prev < 0, blocks, prev)
        idx_v[nz + n : nz + n + 1, :] = jnp.where(last < 0, blocks, last)
    for at, table in ((6, rows), (7, sends)):
        last = jnp.full((1, 128), coups, I32)
        for k in range(coups):
            last = jnp.where(lane == table[0, k], k, last)
        idx_v[at : at + 1, :] = last
    idx_copy = pltpu.make_async_copy(idx_v, idx, idx_sem)
    idx_copy.start()

    zero_block = jnp.zeros((width, block), F32)
    for chain in chains:
        chain[blocks] = zero_block
    coup[coups] = zero_block
    cheb = cheb_ref[...]
    cheb_all = jnp.concatenate([cheb[k].T for k in range(4)], axis=1)

    def lanes(i):
        return pl.ds(pl.multiple_of(i * block, block), block)

    def forward_copy(at, level):
        pair = pl.ds(2 * level, 2)
        return pltpu.make_async_remote_copy(
            src_ref=send_f.at[at, pair], dst_ref=recv_f.at[at, pair],
            send_sem=sf_sem.at[at, level], recv_sem=rf_sem.at[at, level],
            device_id=(partner(level),), device_id_type=MESH,
        )

    def adjoint_copy(at, level):
        pair = pl.ds(2 * level, 2)
        return pltpu.make_async_remote_copy(
            src_ref=send_b.at[at, pair], dst_ref=recv_b.at[at, pair],
            send_sem=sb_sem.at[at, level], recv_sem=rb_sem.at[at, level],
            device_id=(partner(level),), device_id_type=MESH,
        )

    def send_forward(at):
        for k in range(coups):
            send_f[at, k] = field[at, sends[0, k]]
        for level in range(rounds):
            forward_copy(at, level).start()

    def send_adjoint(at):
        for k in range(coups):
            term = dot(back[at, rows[0, k]], cross[0, k // 2, k % 2])
            send_b[at, k] = (term * pair_ref[0, k // 2].astype(F32)).astype(BF16)
        for level in range(rounds):
            adjoint_copy(at, level).start()

    def take_forward(at):
        for level in range(rounds):
            forward_copy(at, level).wait_recv()
        for k in range(coups):
            term = dot(recv_f[at, k], cross_t[k]) * pair_ref[0, k // 2].astype(F32)
            coup[k] = term + coup[rows[1, k]]

    def take_adjoint(at):
        for level in range(rounds):
            adjoint_copy(at, level).wait_recv()
        for k in range(coups):
            coup[k] = recv_b[at, k].astype(F32) + coup[sends[1, k]]

    def forward_rows(at, low, high, fresh, unroll):
        def body(i, carry):
            values = jnp.concatenate([field[at, col[i, n]] for n in range(nz)], axis=1)
            if fresh:
                tiles = []
                for n in range(nz):
                    tile = lap[i, n].T
                    lap_t[i, n] = tile
                    tiles.append(tile)
            else:
                tiles = [lap_t[i, n] for n in range(nz)]
            summed = dot(values, jnp.concatenate(tiles, axis=0)) + coup[idx[6, i]]
            if at > 0:
                summed = 2.0 * summed - field[at - 1, i].astype(F32)
            field[at + 1, i] = (summed * mask_of(i)).astype(BF16)
            return carry

        lax.fori_loop(low, high, body, 0, unroll=unroll)

    def adjoint_chains(at):
        def body(i, carry):
            tiles = jnp.concatenate([lap[i, n] for n in range(nz)], axis=1)
            terms = dot(back[at, i], tiles)
            for n in range(nz):
                chains[n][i] = terms[:, n * block : (n + 1) * block] + chains[n][idx[n, i]]
            return carry

        lax.fori_loop(0, blocks, body, 0, unroll=16)

    def adjoint_sums(at):
        def body(i, carry):
            summed = coup[idx[7, i]]
            for n in range(nz):
                summed = summed + chains[n][idx[nz + n, i]]
            lifted = dot(cheb_ref[2 - at], up[i])
            if at < 2:
                summed = lifted + 2.0 * summed
            else:
                summed = lifted + summed
            if at > 0:
                summed = summed - back[at - 1, i].astype(F32)
            summed = (summed * mask_of(i)).astype(BF16)
            if at < 2:
                back[at + 1, i] = summed
            else:
                gradx[:, lanes(i)] = summed
            return carry

        lax.fori_loop(0, blocks, body, 0, unroll=8)

    loads[0].wait()

    def zeroth_body(i, carry):
        field[0, i] = feat[:, lanes(i)] * mask_of(i).astype(BF16)
        return carry

    lax.fori_loop(0, blocks, zeroth_body, 0, unroll=8)
    pl.semaphore_wait(barrier, rounds + GROUP - 1 + far_size - 1)
    send_forward(0)

    loads[1].wait()

    def upstream_body(i, carry):
        value = cot[:, lanes(i)] * mask_of(i).astype(BF16)
        up[i] = value
        up_t[i] = value.T
        back[0, i] = (dot(cheb_ref[3], value) * mask_of(i)).astype(BF16)
        return carry

    lax.fori_loop(0, blocks, upstream_body, 0, unroll=8)
    loads[2].wait()
    for k in range(coups):
        cross_t[k] = cross[0, k // 2, k % 2].T
    send_adjoint(0)
    idx_copy.wait()

    take_forward(0)
    for part_at in range(CHUNKS):
        lap_load(part_at).wait()
        forward_rows(0, part_at * per, (part_at + 1) * per, True, per)
    send_forward(1)
    adjoint_chains(0)
    take_adjoint(0)
    adjoint_sums(0)
    send_adjoint(1)
    take_forward(1)
    forward_rows(1, 0, blocks, False, 16)
    send_forward(2)
    adjoint_chains(1)
    take_adjoint(1)
    adjoint_sums(1)
    send_adjoint(2)
    take_forward(2)
    forward_rows(2, 0, blocks, False, 16)

    def weight_body(i, total):
        values = jnp.concatenate(
            [jnp.concatenate([field[k, 2 * i + h] for k in range(4)], axis=0) for h in range(2)], axis=1
        )
        ups = jnp.concatenate([up_t[2 * i + h] for h in range(2)], axis=0)
        return total + dot(values, ups)

    total = lax.fori_loop(0, blocks // 2, weight_body, jnp.zeros((4 * width, width), F32), unroll=4)
    half = 2 * width
    part[...] = jnp.concatenate([total[:half], total[half:]], axis=1)

    def near_copy(step, source, target, ssem, rsem, spread):
        peer_at = (near + step) % GROUP
        src = source.at[pl.ds(pl.multiple_of(peer_at * 8, 8), 8)] if spread else source
        return pltpu.make_async_remote_copy(
            src_ref=src, dst_ref=target.at[near], send_sem=ssem.at[step], recv_sem=rsem.at[near],
            device_id=(near_peer(step),), device_id_type=MESH,
        )

    def far_copy(step):
        return pltpu.make_async_remote_copy(
            src_ref=mine2, dst_ref=got2.at[far], send_sem=s2_sem.at[step], recv_sem=r2_sem.at[far],
            device_id=(far_peer(step),), device_id_type=MESH,
        )

    def arrival(source, target, at, ssem, rsem, peer):
        return pltpu.make_async_remote_copy(
            src_ref=source, dst_ref=target.at[at], send_sem=ssem.at[0], recv_sem=rsem.at[at],
            device_id=(peer,), device_id_type=MESH,
        )

    @pl.loop(1, GROUP)
    def _(step):
        near_copy(step, part, got1, s1_sem, r1_sem, True).start()

    got1[near] = part[pl.ds(pl.multiple_of(near * 8, 8), 8), :]

    def output_body(i, carry):
        values = jnp.concatenate([field[k, i] for k in range(4)], axis=0)
        conv[:, lanes(i)] = (dot(cheb_all, values) * mask_of(i)).astype(BF16)
        return carry

    lax.fori_loop(0, blocks, output_body, 0, unroll=8)
    conv_out = pltpu.make_async_copy(conv, conv_hbm, out_sem.at[0])
    conv_out.start()

    @pl.loop(1, GROUP)
    def _(step):
        arrival(part.at[pl.ds(0, 8)], got1, (near + step) % GROUP, s1_sem, r1_sem, near_peer(step)).wait_recv()

    summed = got1[0]
    for at in range(1, GROUP):
        summed = summed + got1[at]
    mine2[...] = summed
    got2[far] = summed
    if far_size > 1:
        @pl.loop(1, far_size)
        def _(step):
            far_copy(step).start()

    adjoint_chains(2)

    if far_size > 1:
        @pl.loop(1, far_size)
        def _(step):
            arrival(mine2, got2, (far + step) % far_size, s2_sem, r2_sem, far_peer(step)).wait_recv()

    summed = got2[0]
    for at in range(1, far_size):
        summed = summed + got2[at]
    mine3[...] = summed
    got3[near] = summed

    @pl.loop(1, GROUP)
    def _(step):
        near_copy(step, mine3, got3, s3_sem, r3_sem, False).start()

    take_adjoint(2)
    adjoint_sums(2)
    gradx_out = pltpu.make_async_copy(gradx, gradx_hbm, out_sem.at[1])
    gradx_out.start()

    @pl.loop(1, GROUP)
    def _(step):
        arrival(mine3, got3, (near + step) % GROUP, s3_sem, r3_sem, near_peer(step)).wait_recv()

    whole = jnp.concatenate([got3[at] for at in range(GROUP)], axis=0)
    whole = jnp.concatenate([whole[:, :width], whole[:, width:]], axis=0)
    for k in range(4):
        gradw_ref[k] = whole[k * width : (k + 1) * width]

    for at in range(3):
        for level in range(rounds):
            forward_copy(at, level).wait_send()
            adjoint_copy(at, level).wait_send()

    @pl.loop(1, GROUP)
    def _(step):
        near_copy(step, part, got1, s1_sem, r1_sem, True).wait_send()
        near_copy(step, mine3, got3, s3_sem, r3_sem, False).wait_send()

    if far_size > 1:
        @pl.loop(1, far_size)
        def _(step):
            far_copy(step).wait_send()

    conv_out.wait()
    gradx_out.wait()


def local(size, features, cheb_weight, lap_tiles, col_index, cross_tiles, send_index, row_index, pair_on, blk_live, cotangent):
    width, pixels = features.shape
    blocks, nz, block = lap_tiles.shape[:3]
    rounds, hb = cross_tiles.shape[1:3]
    coups = rounds * hb
    hbm = pl.BlockSpec(memory_space=pl.ANY)
    smem = pl.BlockSpec(memory_space=pltpu.SMEM)
    vmem = pl.BlockSpec(memory_space=pltpu.VMEM)
    dma = pltpu.SemaphoreType.DMA
    far_size = size // GROUP
    return pl.pallas_call(
        functools.partial(kernel, size),
        out_shape=(
            jax.ShapeDtypeStruct((width, pixels), BF16),
            jax.ShapeDtypeStruct((width, pixels), BF16),
            jax.ShapeDtypeStruct(cheb_weight.shape, F32),
        ),
        in_specs=[hbm, vmem, hbm, vmem, smem, hbm, smem, smem, smem, smem, hbm],
        out_specs=(hbm, hbm, vmem),
        scratch_shapes=[
            pltpu.VMEM((width, pixels), BF16),
            pltpu.VMEM((width, pixels), BF16),
            pltpu.VMEM((blocks, nz, block, block), BF16),
            pltpu.VMEM((blocks, nz, block, block), BF16),
            pltpu.VMEM((1, rounds, hb, block, block), BF16),
            pltpu.VMEM((coups, block, block), BF16),
            pltpu.VMEM((4, blocks, width, block), BF16),
            pltpu.VMEM((3, blocks, width, block), BF16),
            pltpu.VMEM((blocks, width, block), BF16),
            pltpu.VMEM((blocks, block, width), BF16),
            pltpu.VMEM((blocks + 1, width, block), F32),
            pltpu.VMEM((blocks + 1, width, block), F32),
            pltpu.VMEM((blocks + 1, width, block), F32),
            pltpu.VMEM((coups + 1, width, block), F32),
            pltpu.VMEM((3, coups, width, block), BF16),
            pltpu.VMEM((3, coups, width, block), BF16),
            pltpu.VMEM((3, coups, width, block), BF16),
            pltpu.VMEM((3, coups, width, block), BF16),
            pltpu.VMEM((width, pixels), BF16),
            pltpu.VMEM((width, pixels), BF16),
            pltpu.VMEM((8, 128), I32),
            pltpu.SMEM((8, 128), I32),
            pltpu.SMEM((2, coups), I32),
            pltpu.SMEM((2, coups), I32),
            pltpu.VMEM((2 * width, 2 * width), F32),
            pltpu.VMEM((GROUP, 8, 2 * width), F32),
            pltpu.VMEM((8, 2 * width), F32),
            pltpu.VMEM((far_size, 8, 2 * width), F32),
            pltpu.VMEM((8, 2 * width), F32),
            pltpu.VMEM((GROUP, 8, 2 * width), F32),
            dma((3,)),
            dma((CHUNKS,)),
            dma,
            dma((2,)),
            dma((3, rounds)),
            dma((3, rounds)),
            dma((3, rounds)),
            dma((3, rounds)),
            dma((GROUP,)),
            dma((GROUP,)),
            dma((far_size,)),
            dma((far_size,)),
            dma((GROUP,)),
            dma((GROUP,)),
        ],
        compiler_params=pltpu.CompilerParams(
            collective_id=0, has_side_effects=True, vmem_limit_bytes=56 * 2**20
        ),
    )(features, cheb_weight, lap_tiles, col_index, col_index, cross_tiles, send_index, row_index, pair_on, blk_live, cotangent)


def solution(mesh):
    dom = P("dom")
    return jax.shard_map(
        functools.partial(local, mesh.shape["dom"]),
        mesh=mesh,
        in_specs=(P(None, "dom"), P(), dom, dom, dom, dom, dom, dom, dom, P(None, "dom")),
        out_specs=(P(None, "dom"), P(None, "dom"), P()),
        check_vma=False,
    )
```

```python
import functools

import jax
import jax.numpy as jnp
from jax import lax
from jax.experimental import pallas as pl
from jax.experimental.pallas import tpu as pltpu
from jax.sharding import PartitionSpec as P

F32 = jnp.float32
BF16 = jnp.bfloat16
I32 = jnp.int32
MESH = pl.DeviceIdType.MESH
GROUP = 16
CHUNKS = 4
FIRST = 16
WIDE = 64
SUMS = 64
DENSE = 64
WEIGHT = 32


def dot(a, b):
    return jnp.dot(a, b, preferred_element_type=F32)


def small_mod(value, count, largest):
    power = 1
    while power * 2 <= largest:
        power *= 2
    while power >= 1:
        step = count * power
        value = jnp.where(value >= step, value - step, value)
        power //= 2
    return value


def kernel(
    size,
    feat_hbm, cheb_ref, lap_hbm, col_vmem, col, cross_hbm, send_ref, row_ref, pair_ref, live_ref, cot_hbm,
    conv_hbm, gradx_hbm, gradw_ref,
    feat, cot, lap, lap_t, cross, cross_t, field0, field1, field2, field3, back0, back1, back2, both_t, chain0, chain1, chain2, coup_f, coup_b,
    send_f, recv_f, send_b, recv_b, conv, gradx, idx_v, idx, sends, rows, part, got1, mine2, got2, mine3, got3,
    load_sem, lap_sem, idx_sem, out_sem, sf_sem, rf_sem, sb_sem, rb_sem,
    s1_sem, r1_sem, s2_sem, r2_sem, s3_sem, r3_sem,
):
    blocks, width, block = lap.shape[0], feat.shape[0], lap.shape[2]
    nz = lap.shape[1]
    rounds = 5
    coups = 2 * rounds
    chains = (chain0, chain1, chain2)
    field = (field0, field1, field2, field3)
    back = (back0, back1, back2)
    me = lax.axis_index("dom")
    near, far = me % GROUP, me // GROUP
    far_size = size // GROUP

    def partner(level):
        bit = (me // (1 << level)) % 2
        return me + (1 << level) * (1 - 2 * bit)

    def near_peer(step):
        return far * GROUP + (near + step) % GROUP

    def far_peer(step):
        return ((far + step) % far_size) * GROUP + near

    per = blocks // CHUNKS
    loads = [
        pltpu.make_async_copy(feat_hbm, feat, load_sem.at[0]),
        pltpu.make_async_copy(cot_hbm, cot, load_sem.at[1]),
        pltpu.make_async_copy(cross_hbm, cross, load_sem.at[2]),
    ]
    for load in loads:
        load.start()

    def lap_load(part_at):
        where = pl.ds(part_at * per, per)
        return pltpu.make_async_copy(lap_hbm.at[where], lap.at[where], lap_sem.at[part_at])

    for part_at in range(CHUNKS):
        lap_load(part_at).start()

    barrier = pltpu.get_barrier_semaphore()
    for level in range(rounds):
        pl.semaphore_signal(barrier, inc=1, device_id=(partner(level),), device_id_type=MESH)

    @pl.loop(1, GROUP)
    def _(step):
        pl.semaphore_signal(barrier, inc=1, device_id=(near_peer(step),), device_id_type=MESH)

    if far_size > 1:
        @pl.loop(1, far_size)
        def _(step):
            pl.semaphore_signal(barrier, inc=1, device_id=(far_peer(step),), device_id_type=MESH)

    live = live_ref[0]

    def mask_of(i):
        return (i < live).astype(F32)

    for k in range(coups):
        sends[0, k] = small_mod(send_ref[0, k % 2, k // 2], live, blocks - 1)
        rows[0, k] = small_mod(row_ref[0, k % 2, k // 2], live, blocks - 1)
    for table in (sends, rows):
        for k in range(coups):
            before = jnp.int32(coups)
            for other in range(k):
                before = jnp.where(table[0, other] == table[0, k], other, before)
            table[1, k] = before
    at_sub = lax.broadcasted_iota(I32, (blocks, blocks), 0)
    at_lane = lax.broadcasted_iota(I32, (blocks, blocks), 1)
    lane = lax.broadcasted_iota(I32, (1, 128), 1)
    for n in range(nz):
        turned = jnp.broadcast_to(col_vmem[n : n + 1, :], (blocks, blocks))
        cols = jnp.sum(jnp.where(at_sub == at_lane, turned, 0), axis=1, keepdims=True)
        same = (cols == turned) & (at_sub < at_lane)
        prev = jnp.max(jnp.where(same, at_sub, -1), axis=0, keepdims=True)
        last = jnp.max(jnp.where(cols == at_lane, at_sub, -1), axis=0, keepdims=True)
        idx_v[n : n + 1, :blocks] = jnp.where(prev < 0, blocks, prev)
        idx_v[nz + n : nz + n + 1, :blocks] = jnp.where(last < 0, blocks, last)
    for at, table in ((6, rows), (7, sends)):
        last = jnp.full((1, 128), coups, I32)
        for k in range(coups):
            last = jnp.where(lane == table[0, k], k, last)
        idx_v[at : at + 1, :] = last
    idx_copy = pltpu.make_async_copy(idx_v, idx, idx_sem)
    idx_copy.start()

    zero_block = jnp.zeros((width, block), F32)
    for chain in chains:
        chain[blocks] = zero_block
    coup_f[coups] = zero_block
    coup_b[coups] = zero_block
    cheb = cheb_ref[...]
    cheb_all = jnp.concatenate([cheb[k].T for k in range(4)], axis=1)
    cheb_back = jnp.concatenate([cheb[k] for k in range(4)], axis=1)

    def lanes(i):
        return pl.ds(pl.multiple_of(i * block, block), block)

    def forward_copy(at, level):
        pair = pl.ds(2 * level, 2)
        return pltpu.make_async_remote_copy(
            src_ref=send_f.at[at, pair], dst_ref=recv_f.at[at, pair],
            send_sem=sf_sem.at[at, level], recv_sem=rf_sem.at[at, level],
            device_id=(partner(level),), device_id_type=MESH,
        )

    def adjoint_copy(at, level):
        pair = pl.ds(2 * level, 2)
        return pltpu.make_async_remote_copy(
            src_ref=send_b.at[at, pair], dst_ref=recv_b.at[at, pair],
            send_sem=sb_sem.at[at, level], recv_sem=rb_sem.at[at, level],
            device_id=(partner(level),), device_id_type=MESH,
        )

    def start_forward(at):
        for level in range(rounds):
            forward_copy(at, level).start()

    def send_adjoint(at, block_of):
        for k in range(coups):
            term = dot(block_of(rows[0, k]), cross[0, k // 2, k % 2])
            send_b[at, k] = (term * pair_ref[0, k // 2].astype(F32)).astype(BF16)
        for level in range(rounds):
            adjoint_copy(at, level).start()

    def take_forward(at):
        for level in range(rounds):
            forward_copy(at, level).wait_recv()
        for k in range(coups):
            term = dot(recv_f[at, k], cross_t[k]) * pair_ref[0, k // 2].astype(F32)
            coup_f[k] = term + coup_f[rows[1, k]]

    def take_adjoint(at):
        for level in range(rounds):
            adjoint_copy(at, level).wait_recv()
        for k in range(coups):
            coup_b[k] = recv_b[at, k].astype(F32) + coup_b[sends[1, k]]

    def forward_value(at, i):
        values = jnp.concatenate([field[at][col[n, i]] for n in range(nz)], axis=1)
        tiles = jnp.concatenate([lap_t[i, n] for n in range(nz)], axis=0)
        summed = dot(values, tiles) + coup_f[idx[6, i]]
        if at > 0:
            summed = 2.0 * summed - field[at - 1][i].astype(F32)
        return (summed * mask_of(i)).astype(BF16)

    def adjoint_value(at, i):
        summed = coup_b[idx[7, i]]
        for n in range(nz):
            summed = summed + chains[n][idx[nz + n, i]]
        if at > 0:
            summed = 2.0 * summed - back[at - 1][i].astype(F32)
        return (summed * mask_of(i)).astype(BF16)

    def adjoint_row(at, i, tiles):
        terms = dot(back[at][i], jnp.concatenate(tiles, axis=1))
        for n in range(nz):
            chains[n][i] = terms[:, n * block : (n + 1) * block] + chains[n][idx[n, i]]

    def first_chains(low):
        def body(step, carry):
            i = low + step
            tiles = [lap[i, n] for n in range(nz)]
            for n in range(nz):
                lap_t[i, n] = tiles[n].T
            adjoint_row(0, i, tiles)
            return carry

        lax.fori_loop(0, per, body, 0, unroll=FIRST)

    def adjoint_chains(at):
        def body(i, carry):
            adjoint_row(at, i, [lap[i, n] for n in range(nz)])
            return carry

        lax.fori_loop(0, blocks, body, 0, unroll=WIDE)

    def forward_rows(at):
        def body(i, carry):
            field[at + 1][i] = forward_value(at, i)
            return carry

        lax.fori_loop(0, blocks, body, 0, unroll=WIDE)

    def send_forward(at):
        for k in range(coups):
            send_f[at, k] = forward_value(at - 1, sends[0, k])
        start_forward(at)

    loads[0].wait()

    def zeroth_body(i, carry):
        field[0][i] = feat[:, lanes(i)] * mask_of(i).astype(BF16)
        return carry

    lax.fori_loop(0, blocks, zeroth_body, 0, unroll=16)
    for k in range(coups):
        send_f[0, k] = field[0][sends[0, k]]
    pl.semaphore_wait(barrier, rounds + GROUP - 1 + far_size - 1)
    start_forward(0)
    loads[1].wait()

    def upstream_body(i, carry):
        back[0][i] = cot[:, lanes(i)] * mask_of(i).astype(BF16)
        return carry

    lax.fori_loop(0, blocks, upstream_body, 0, unroll=16)
    loads[2].wait()
    send_adjoint(0, lambda i: back[0][i])
    for k in range(coups):
        cross_t[k] = cross[0, k // 2, k % 2].T
    idx_copy.wait()

    @pl.loop(0, CHUNKS)
    def _(part_at):
        lap_load(part_at).wait()
        first_chains(part_at * per)

    take_forward(0)
    send_forward(1)

    forward_rows(0)
    take_adjoint(0)
    send_adjoint(1, lambda i: adjoint_value(0, i))

    def adjoint_first_body(i, total):
        value = adjoint_value(0, i)
        back[1][i] = value
        turned = jnp.concatenate([back[0][i], value], axis=0).T
        both_t[i] = turned
        return total + dot(jnp.concatenate([field[0][i], field[1][i]], axis=0), turned)

    low = lax.fori_loop(0, blocks, adjoint_first_body, jnp.zeros((2 * width, 2 * width), F32), unroll=SUMS)
    adjoint_chains(1)
    take_forward(1)
    send_forward(2)

    forward_rows(1)

    def second_terms(i, total):
        values = jnp.concatenate([field[2][2 * i + h] for h in range(2)], axis=1)
        return total + dot(values, jnp.concatenate([both_t[2 * i + h] for h in range(2)], axis=0))

    zero = jnp.zeros((width, 2 * width), F32)
    high = lax.fori_loop(0, blocks // 2, second_terms, zero, unroll=WEIGHT)

    last_term = 2.0 * high[:, width:] - low[width:, :width]
    part[...] = jnp.concatenate([low[:, :width], jnp.concatenate([high[:, :width], last_term], axis=0)], axis=1)

    def near_copy(step, source, target, ssem, rsem, spread):
        peer_at = (near + step) % GROUP
        src = source.at[pl.ds(pl.multiple_of(peer_at * 8, 8), 8)] if spread else source
        return pltpu.make_async_remote_copy(
            src_ref=src, dst_ref=target.at[near], send_sem=ssem.at[step], recv_sem=rsem.at[near],
            device_id=(near_peer(step),), device_id_type=MESH,
        )

    def far_copy(step):
        return pltpu.make_async_remote_copy(
            src_ref=mine2, dst_ref=got2.at[far], send_sem=s2_sem.at[step], recv_sem=r2_sem.at[far],
            device_id=(far_peer(step),), device_id_type=MESH,
        )

    def arrival(source, target, at, ssem, rsem, peer):
        return pltpu.make_async_remote_copy(
            src_ref=source, dst_ref=target.at[at], send_sem=ssem.at[0], recv_sem=rsem.at[at],
            device_id=(peer,), device_id_type=MESH,
        )

    @pl.loop(1, GROUP)
    def _(step):
        near_copy(step, part, got1, s1_sem, r1_sem, True).start()

    got1[near] = part[pl.ds(pl.multiple_of(near * 8, 8), 8), :]
    take_adjoint(1)
    send_adjoint(2, lambda i: adjoint_value(1, i))

    def adjoint_second_body(i, carry):
        back[2][i] = adjoint_value(1, i)
        return carry

    lax.fori_loop(0, blocks, adjoint_second_body, 0, unroll=SUMS)
    adjoint_chains(2)
    take_forward(2)

    forward_rows(2)

    @pl.loop(1, GROUP)
    def _(step):
        arrival(part.at[pl.ds(0, 8)], got1, (near + step) % GROUP, s1_sem, r1_sem, near_peer(step)).wait_recv()

    summed = got1[0]
    for at in range(1, GROUP):
        summed = summed + got1[at]
    mine2[...] = summed
    got2[far] = summed
    if far_size > 1:
        @pl.loop(1, far_size)
        def _(step):
            far_copy(step).start()


    def output_body(i, carry):
        values = jnp.concatenate([field[k][i] for k in range(4)], axis=0)
        conv[:, lanes(i)] = (dot(cheb_all, values) * mask_of(i)).astype(BF16)
        return carry

    lax.fori_loop(0, blocks, output_body, 0, unroll=DENSE)
    conv_out = pltpu.make_async_copy(conv, conv_hbm, out_sem.at[0])
    conv_out.start()
    take_adjoint(2)

    def gradient_body(i, carry):
        third = adjoint_value(2, i)
        values = jnp.concatenate([back[0][i], back[1][i], back[2][i], third], axis=0)
        gradx[:, lanes(i)] = (dot(cheb_back, values) * mask_of(i)).astype(BF16)
        return carry

    lax.fori_loop(0, blocks, gradient_body, 0, unroll=DENSE)
    gradx_out = pltpu.make_async_copy(gradx, gradx_hbm, out_sem.at[1])
    gradx_out.start()

    if far_size > 1:
        @pl.loop(1, far_size)
        def _(step):
            arrival(mine2, got2, (far + step) % far_size, s2_sem, r2_sem, far_peer(step)).wait_recv()

    summed = got2[0]
    for at in range(1, far_size):
        summed = summed + got2[at]
    mine3[...] = summed
    got3[near] = summed

    @pl.loop(1, GROUP)
    def _(step):
        near_copy(step, mine3, got3, s3_sem, r3_sem, False).start()

    @pl.loop(1, GROUP)
    def _(step):
        arrival(mine3, got3, (near + step) % GROUP, s3_sem, r3_sem, near_peer(step)).wait_recv()

    whole = jnp.concatenate([got3[at] for at in range(GROUP)], axis=0)
    whole = jnp.concatenate([whole[:, :width], whole[:, width:]], axis=0)
    for k in range(4):
        gradw_ref[k] = whole[k * width : (k + 1) * width]

    for at in range(3):
        for level in range(rounds):
            forward_copy(at, level).wait_send()
            adjoint_copy(at, level).wait_send()

    @pl.loop(1, GROUP)
    def _(step):
        near_copy(step, part, got1, s1_sem, r1_sem, True).wait_send()
        near_copy(step, mine3, got3, s3_sem, r3_sem, False).wait_send()

    if far_size > 1:
        @pl.loop(1, far_size)
        def _(step):
            far_copy(step).wait_send()

    conv_out.wait()
    gradx_out.wait()


PIECES = 4


def handed_on(conv_in, gradx_in, gradw_in, conv_out, gradx_out, gradw_out, conv, gradx, gradw, in_sem, out_sem):
    moves = []
    for at, (source, held, target) in enumerate(
        ((gradw_in, gradw, gradw_out), (conv_in, conv, conv_out), (gradx_in, gradx, gradx_out))
    ):
        each = source.shape[0] // PIECES
        for piece in range(PIECES):
            where = pl.ds(piece * each, each)
            moves.append(
                (
                    pltpu.make_async_copy(source.at[where], held.at[where], in_sem.at[at, piece]),
                    pltpu.make_async_copy(held.at[where], target.at[where], out_sem.at[at, piece]),
                )
            )
    for first, _ in moves:
        first.start()
    for first, second in moves:
        first.wait()
        second.start()
    for _, second in moves:
        second.wait()


def local(size, features, cheb_weight, lap_tiles, col_index, cross_tiles, send_index, row_index, pair_on, blk_live, cotangent):
    width, pixels = features.shape
    blocks, nz, block = lap_tiles.shape[:3]
    rounds, hb = cross_tiles.shape[1:3]
    coups = rounds * hb
    hbm = pl.BlockSpec(memory_space=pl.ANY)
    smem = pl.BlockSpec(memory_space=pltpu.SMEM)
    vmem = pl.BlockSpec(memory_space=pltpu.VMEM)
    dma = pltpu.SemaphoreType.DMA
    far_size = size // GROUP
    results = pl.pallas_call(
        functools.partial(kernel, size),
        out_shape=(
            jax.ShapeDtypeStruct((width, pixels), BF16),
            jax.ShapeDtypeStruct((width, pixels), BF16),
            jax.ShapeDtypeStruct(cheb_weight.shape, F32),
        ),
        in_specs=[hbm, vmem, hbm, vmem, smem, hbm, smem, smem, smem, smem, hbm],
        out_specs=(hbm, hbm, vmem),
        scratch_shapes=[
            pltpu.VMEM((width, pixels), BF16),
            pltpu.VMEM((width, pixels), BF16),
            pltpu.VMEM((blocks, nz, block, block), BF16),
            pltpu.VMEM((blocks, nz, block, block), BF16),
            pltpu.VMEM((1, rounds, hb, block, block), BF16),
            pltpu.VMEM((coups, block, block), BF16),
            *[pltpu.VMEM((blocks, width, block), BF16)] * 7,
            pltpu.VMEM((blocks, block, 2 * width), BF16),
            pltpu.VMEM((blocks + 1, width, block), F32),
            pltpu.VMEM((blocks + 1, width, block), F32),
            pltpu.VMEM((blocks + 1, width, block), F32),
            pltpu.VMEM((coups + 1, width, block), F32),
            pltpu.VMEM((coups + 1, width, block), F32),
            pltpu.VMEM((3, coups, width, block), BF16),
            pltpu.VMEM((3, coups, width, block), BF16),
            pltpu.VMEM((3, coups, width, block), BF16),
            pltpu.VMEM((3, coups, width, block), BF16),
            pltpu.VMEM((width, pixels), BF16),
            pltpu.VMEM((width, pixels), BF16),
            pltpu.VMEM((8, 128), I32),
            pltpu.SMEM((8, 128), I32),
            pltpu.SMEM((2, coups), I32),
            pltpu.SMEM((2, coups), I32),
            pltpu.VMEM((2 * width, 2 * width), F32),
            pltpu.VMEM((GROUP, 8, 2 * width), F32),
            pltpu.VMEM((8, 2 * width), F32),
            pltpu.VMEM((far_size, 8, 2 * width), F32),
            pltpu.VMEM((8, 2 * width), F32),
            pltpu.VMEM((GROUP, 8, 2 * width), F32),
            dma((3,)),
            dma((CHUNKS,)),
            dma,
            dma((2,)),
            dma((3, rounds)),
            dma((3, rounds)),
            dma((3, rounds)),
            dma((3, rounds)),
            dma((GROUP,)),
            dma((GROUP,)),
            dma((far_size,)),
            dma((far_size,)),
            dma((GROUP,)),
            dma((GROUP,)),
        ],
        compiler_params=pltpu.CompilerParams(
            collective_id=0, has_side_effects=True, vmem_limit_bytes=56 * 2**20
        ),
    )(features, cheb_weight, lap_tiles, col_index.T, col_index.T, cross_tiles, send_index.swapaxes(1, 2), row_index.swapaxes(1, 2), pair_on, blk_live, cotangent)
    return pl.pallas_call(
        handed_on,
        out_shape=tuple(jax.ShapeDtypeStruct(each.shape, each.dtype) for each in results),
        in_specs=[hbm] * 3,
        out_specs=(hbm,) * 3,
        scratch_shapes=[pltpu.VMEM(each.shape, each.dtype) for each in results] + [dma((3, PIECES)), dma((3, PIECES))],
    )(*results)


def solution(mesh):
    dom = P("dom")
    return jax.shard_map(
        functools.partial(local, mesh.shape["dom"]),
        mesh=mesh,
        in_specs=(P(None, "dom"), P(), dom, dom, dom, dom, dom, dom, dom, P(None, "dom")),
        out_specs=(P(None, "dom"), P(None, "dom"), P()),
        check_vma=False,
    )
```

```python
import functools

import jax
import jax.numpy as jnp
from jax import lax
from jax.experimental import pallas as pl
from jax.experimental.pallas import tpu as pltpu
from jax.sharding import PartitionSpec as P

F32 = jnp.float32
BF16 = jnp.bfloat16
I32 = jnp.int32
MESH = pl.DeviceIdType.MESH
GROUP = 16
CHUNKS = 4
FIRST = 16
WIDE = 64
SUMS = 64
DENSE = 64
WEIGHT = 32


def dot(a, b):
    return jnp.dot(a, b, preferred_element_type=F32)


def small_mod(value, count, largest):
    power = 1
    while power * 2 <= largest:
        power *= 2
    while power >= 1:
        step = count * power
        value = jnp.where(value >= step, value - step, value)
        power //= 2
    return value


def kernel(
    size,
    feat_hbm, cheb_ref, lap_hbm, col_vmem, col, cross_hbm, send_ref, row_ref, pair_ref, live_ref, cot_hbm,
    conv_hbm, gradx_hbm, gradw_ref,
    feat, cot, lap, lap_t, cross, cross_t, field0, field1, field2, field3, back0, back1, back2, both_t, chain0, chain1, chain2, coup_f, coup_b,
    send_f, recv_f, send_b, recv_b, conv, gradx, idx_v, idx, sends, rows, part, got1, mine2, got2, mine3, got3,
    load_sem, lap_sem, idx_sem, out_sem, sf_sem, rf_sem, sb_sem, rb_sem,
    s1_sem, r1_sem, s2_sem, r2_sem, s3_sem, r3_sem,
):
    blocks, width, block = lap.shape[0], feat.shape[0], lap.shape[2]
    nz = lap.shape[1]
    rounds = 5
    coups = 2 * rounds
    chains = (chain0, chain1, chain2)
    field = (field0, field1, field2, field3)
    back = (back0, back1, back2)
    me = lax.axis_index("dom")
    near, far = me % GROUP, me // GROUP
    far_size = size // GROUP

    def partner(level):
        bit = (me // (1 << level)) % 2
        return me + (1 << level) * (1 - 2 * bit)

    def near_peer(step):
        return far * GROUP + (near + step) % GROUP

    def far_peer(step):
        return ((far + step) % far_size) * GROUP + near

    per = blocks // CHUNKS
    loads = [
        pltpu.make_async_copy(feat_hbm, feat, load_sem.at[0]),
        pltpu.make_async_copy(cot_hbm, cot, load_sem.at[1]),
        pltpu.make_async_copy(cross_hbm, cross, load_sem.at[2]),
    ]
    for load in loads:
        load.start()

    def lap_load(part_at):
        where = pl.ds(part_at * per, per)
        return pltpu.make_async_copy(lap_hbm.at[where], lap.at[where], lap_sem.at[part_at])

    for part_at in range(CHUNKS):
        lap_load(part_at).start()

    barrier = pltpu.get_barrier_semaphore()
    for level in range(rounds):
        pl.semaphore_signal(barrier, inc=1, device_id=(partner(level),), device_id_type=MESH)

    @pl.loop(1, GROUP, unroll=True)
    def _(step):
        pl.semaphore_signal(barrier, inc=1, device_id=(near_peer(step),), device_id_type=MESH)

    if far_size > 1:
        @pl.loop(1, far_size, unroll=True)
        def _(step):
            pl.semaphore_signal(barrier, inc=1, device_id=(far_peer(step),), device_id_type=MESH)

    live = live_ref[0]

    def mask_of(i):
        return (i < live).astype(F32)

    for k in range(coups):
        sends[0, k] = small_mod(send_ref[0, k % 2, k // 2], live, blocks - 1)
        rows[0, k] = small_mod(row_ref[0, k % 2, k // 2], live, blocks - 1)
    for table in (sends, rows):
        for k in range(coups):
            before = jnp.int32(coups)
            for other in range(k):
                before = jnp.where(table[0, other] == table[0, k], other, before)
            table[1, k] = before
    at_sub = lax.broadcasted_iota(I32, (blocks, blocks), 0)
    at_lane = lax.broadcasted_iota(I32, (blocks, blocks), 1)
    lane = lax.broadcasted_iota(I32, (1, 128), 1)
    for n in range(nz):
        turned = jnp.broadcast_to(col_vmem[n : n + 1, :], (blocks, blocks))
        cols = jnp.sum(jnp.where(at_sub == at_lane, turned, 0), axis=1, keepdims=True)
        same = (cols == turned) & (at_sub < at_lane)
        prev = jnp.max(jnp.where(same, at_sub, -1), axis=0, keepdims=True)
        last = jnp.max(jnp.where(cols == at_lane, at_sub, -1), axis=0, keepdims=True)
        idx_v[n : n + 1, :blocks] = jnp.where(prev < 0, blocks, prev)
        idx_v[nz + n : nz + n + 1, :blocks] = jnp.where(last < 0, blocks, last)
    for at, table in ((6, rows), (7, sends)):
        last = jnp.full((1, 128), coups, I32)
        for k in range(coups):
            last = jnp.where(lane == table[0, k], k, last)
        idx_v[at : at + 1, :] = last
    idx_copy = pltpu.make_async_copy(idx_v, idx, idx_sem)
    idx_copy.start()

    zero_block = jnp.zeros((width, block), F32)
    for chain in chains:
        chain[blocks] = zero_block
    coup_f[coups] = zero_block
    coup_b[coups] = zero_block
    cheb = cheb_ref[...]
    cheb_all = jnp.concatenate([cheb[k].T for k in range(4)], axis=1)
    cheb_back = jnp.concatenate([cheb[k] for k in range(4)], axis=1)

    def lanes(i):
        return pl.ds(pl.multiple_of(i * block, block), block)

    def forward_copy(at, level):
        pair = pl.ds(2 * level, 2)
        return pltpu.make_async_remote_copy(
            src_ref=send_f.at[at, pair], dst_ref=recv_f.at[at, pair],
            send_sem=sf_sem.at[at], recv_sem=rf_sem.at[at],
            device_id=(partner(level),), device_id_type=MESH,
        )

    def adjoint_copy(at, level):
        pair = pl.ds(2 * level, 2)
        return pltpu.make_async_remote_copy(
            src_ref=send_b.at[at, pair], dst_ref=recv_b.at[at, pair],
            send_sem=sb_sem.at[at], recv_sem=rb_sem.at[at],
            device_id=(partner(level),), device_id_type=MESH,
        )

    def all_of(source, target, ssem, rsem):
        return pltpu.make_async_remote_copy(
            src_ref=source, dst_ref=target, send_sem=ssem, recv_sem=rsem,
            device_id=(partner(0),), device_id_type=MESH,
        )

    def all_forward(at):
        return all_of(send_f.at[at], recv_f.at[at], sf_sem.at[at], rf_sem.at[at])

    def all_adjoint(at):
        return all_of(send_b.at[at], recv_b.at[at], sb_sem.at[at], rb_sem.at[at])

    def start_forward(at):
        for level in (4, 2, 3, 1, 0):
            forward_copy(at, level).start()

    def send_adjoint(at, block_of):
        for k in range(coups):
            term = dot(block_of(rows[0, k]), cross[0, k // 2, k % 2])
            send_b[at, k] = (term * pair_ref[0, k // 2].astype(F32)).astype(BF16)
        for level in (4, 2, 3, 1, 0):
            adjoint_copy(at, level).start()

    def take_forward(at):
        all_forward(at).wait_recv()
        for k in range(coups):
            term = dot(recv_f[at, k], cross_t[k]) * pair_ref[0, k // 2].astype(F32)
            coup_f[k] = term + coup_f[rows[1, k]]

    def take_adjoint(at):
        all_adjoint(at).wait_recv()
        for k in range(coups):
            coup_b[k] = recv_b[at, k].astype(F32) + coup_b[sends[1, k]]

    def forward_value(at, i):
        values = jnp.concatenate([field[at][col[n, i]] for n in range(nz)], axis=1)
        tiles = jnp.concatenate([lap_t[i, n] for n in range(nz)], axis=0)
        summed = dot(values, tiles) + coup_f[idx[6, i]]
        if at > 0:
            summed = 2.0 * summed - field[at - 1][i].astype(F32)
        return (summed * mask_of(i)).astype(BF16)

    def adjoint_value(at, i):
        summed = coup_b[idx[7, i]]
        for n in range(nz):
            summed = summed + chains[n][idx[nz + n, i]]
        if at > 0:
            summed = 2.0 * summed - back[at - 1][i].astype(F32)
        return (summed * mask_of(i)).astype(BF16)

    def adjoint_row(at, i, tiles):
        terms = dot(back[at][i], jnp.concatenate(tiles, axis=1))
        for n in range(nz):
            chains[n][i] = terms[:, n * block : (n + 1) * block] + chains[n][idx[n, i]]

    def first_chains(low):
        def body(step, carry):
            i = low + step
            tiles = [lap[i, n] for n in range(nz)]
            for n in range(nz):
                lap_t[i, n] = tiles[n].T
            adjoint_row(0, i, tiles)
            return carry

        lax.fori_loop(0, per, body, 0, unroll=FIRST)

    def adjoint_chains(at):
        def body(i, carry):
            adjoint_row(at, i, [lap[i, n] for n in range(nz)])
            return carry

        lax.fori_loop(0, blocks, body, 0, unroll=WIDE)

    def forward_rows(at):
        def body(i, carry):
            field[at + 1][i] = forward_value(at, i)
            return carry

        lax.fori_loop(0, blocks, body, 0, unroll=WIDE)

    def send_forward(at):
        for k in range(coups):
            send_f[at, k] = forward_value(at - 1, sends[0, k])
        start_forward(at)

    loads[0].wait()

    def zeroth_body(i, carry):
        field[0][i] = feat[:, lanes(i)] * mask_of(i).astype(BF16)
        return carry

    lax.fori_loop(0, blocks, zeroth_body, 0, unroll=16)
    for k in range(coups):
        send_f[0, k] = field[0][sends[0, k]]
    pl.semaphore_wait(barrier, rounds + GROUP - 1 + far_size - 1)
    start_forward(0)
    loads[1].wait()

    def upstream_body(i, carry):
        back[0][i] = cot[:, lanes(i)] * mask_of(i).astype(BF16)
        return carry

    lax.fori_loop(0, blocks, upstream_body, 0, unroll=16)
    loads[2].wait()
    send_adjoint(0, lambda i: back[0][i])
    for k in range(coups):
        cross_t[k] = cross[0, k // 2, k % 2].T
    idx_copy.wait()

    @pl.loop(0, CHUNKS)
    def _(part_at):
        lap_load(part_at).wait()
        first_chains(part_at * per)

    take_forward(0)
    send_forward(1)

    forward_rows(0)
    take_adjoint(0)
    send_adjoint(1, lambda i: adjoint_value(0, i))

    def adjoint_first_body(i, total):
        value = adjoint_value(0, i)
        back[1][i] = value
        turned = jnp.concatenate([back[0][i], value], axis=0).T
        both_t[i] = turned
        return total + dot(jnp.concatenate([field[0][i], field[1][i]], axis=0), turned)

    low = lax.fori_loop(0, blocks, adjoint_first_body, jnp.zeros((2 * width, 2 * width), F32), unroll=SUMS)
    adjoint_chains(1)
    take_forward(1)
    send_forward(2)

    forward_rows(1)

    def second_terms(i, total):
        values = jnp.concatenate([field[2][2 * i + h] for h in range(2)], axis=1)
        return total + dot(values, jnp.concatenate([both_t[2 * i + h] for h in range(2)], axis=0))

    zero = jnp.zeros((width, 2 * width), F32)
    high = lax.fori_loop(0, blocks // 2, second_terms, zero, unroll=WEIGHT)

    last_term = 2.0 * high[:, width:] - low[width:, :width]
    part[...] = jnp.concatenate([low[:, :width], jnp.concatenate([high[:, :width], last_term], axis=0)], axis=1)

    def near_copy(step, source, target, ssem, rsem, spread):
        peer_at = (near + step) % GROUP
        src = source.at[pl.ds(pl.multiple_of(peer_at * 8, 8), 8)] if spread else source
        return pltpu.make_async_remote_copy(
            src_ref=src, dst_ref=target.at[near], send_sem=ssem, recv_sem=rsem,
            device_id=(near_peer(step),), device_id_type=MESH,
        )

    def far_copy(step):
        return pltpu.make_async_remote_copy(
            src_ref=mine2, dst_ref=got2.at[far], send_sem=s2_sem, recv_sem=r2_sem,
            device_id=(far_peer(step),), device_id_type=MESH,
        )

    def slots(target, ssem, rsem):
        most = target.at[pl.ds(0, target.shape[0] - 1)]
        return all_of(most, most, ssem, rsem)

    @pl.loop(0, GROUP - 1, unroll=True)
    def _(at):
        near_copy(1 + (at + GROUP // 2 - 1) % (GROUP - 1), part, got1, s1_sem, r1_sem, True).start()

    got1[near] = part[pl.ds(pl.multiple_of(near * 8, 8), 8), :]
    take_adjoint(1)
    send_adjoint(2, lambda i: adjoint_value(1, i))

    def adjoint_second_body(i, carry):
        back[2][i] = adjoint_value(1, i)
        return carry

    lax.fori_loop(0, blocks, adjoint_second_body, 0, unroll=SUMS)
    adjoint_chains(2)
    take_forward(2)

    forward_rows(2)

    slots(got1, s1_sem, r1_sem).wait_recv()
    summed = got1[0]
    for at in range(1, GROUP):
        summed = summed + got1[at]
    mine2[...] = summed
    got2[far] = summed
    if far_size > 1:
        @pl.loop(0, far_size - 1, unroll=True)
        def _(at):
            far_copy(1 + (at + far_size // 2 - 1) % (far_size - 1)).start()


    def output_body(i, carry):
        values = jnp.concatenate([field[k][i] for k in range(4)], axis=0)
        conv[:, lanes(i)] = (dot(cheb_all, values) * mask_of(i)).astype(BF16)
        return carry

    lax.fori_loop(0, blocks, output_body, 0, unroll=DENSE)
    conv_out = pltpu.make_async_copy(conv, conv_hbm, out_sem.at[0])
    conv_out.start()
    take_adjoint(2)

    def gradient_body(i, carry):
        third = adjoint_value(2, i)
        values = jnp.concatenate([back[0][i], back[1][i], back[2][i], third], axis=0)
        gradx[:, lanes(i)] = (dot(cheb_back, values) * mask_of(i)).astype(BF16)
        return carry

    lax.fori_loop(0, blocks, gradient_body, 0, unroll=DENSE)
    gradx_out = pltpu.make_async_copy(gradx, gradx_hbm, out_sem.at[1])
    gradx_out.start()

    if far_size > 1:
        slots(got2, s2_sem, r2_sem).wait_recv()

    summed = got2[0]
    for at in range(1, far_size):
        summed = summed + got2[at]
    mine3[...] = summed
    got3[near] = summed

    @pl.loop(0, GROUP - 1, unroll=True)
    def _(at):
        near_copy(1 + (at + GROUP // 2 - 1) % (GROUP - 1), mine3, got3, s3_sem, r3_sem, False).start()

    slots(got3, s3_sem, r3_sem).wait_recv()
    whole = jnp.concatenate([got3[at] for at in range(GROUP)], axis=0)
    whole = jnp.concatenate([whole[:, :width], whole[:, width:]], axis=0)
    for k in range(4):
        gradw_ref[k] = whole[k * width : (k + 1) * width]

    for at in range(3):
        all_forward(at).wait_send()
        all_adjoint(at).wait_send()

    slots(got1, s1_sem, r1_sem).wait_send()
    slots(got3, s3_sem, r3_sem).wait_send()
    if far_size > 1:
        slots(got2, s2_sem, r2_sem).wait_send()

    conv_out.wait()
    gradx_out.wait()


PIECES = 4


def handed_on(conv_in, gradx_in, gradw_in, conv_out, gradx_out, gradw_out, conv, gradx, gradw, in_sem, out_sem):
    moves = []
    for at, (source, held, target) in enumerate(
        ((gradw_in, gradw, gradw_out), (conv_in, conv, conv_out), (gradx_in, gradx, gradx_out))
    ):
        each = source.shape[0] // PIECES
        for piece in range(PIECES):
            where = pl.ds(piece * each, each)
            moves.append(
                (
                    pltpu.make_async_copy(source.at[where], held.at[where], in_sem.at[at, piece]),
                    pltpu.make_async_copy(held.at[where], target.at[where], out_sem.at[at, piece]),
                )
            )
    for first, _ in moves:
        first.start()
    for first, second in moves:
        first.wait()
        second.start()
    for _, second in moves:
        second.wait()


def local(size, features, cheb_weight, lap_tiles, col_index, cross_tiles, send_index, row_index, pair_on, blk_live, cotangent):
    width, pixels = features.shape
    blocks, nz, block = lap_tiles.shape[:3]
    rounds, hb = cross_tiles.shape[1:3]
    coups = rounds * hb
    hbm = pl.BlockSpec(memory_space=pl.ANY)
    smem = pl.BlockSpec(memory_space=pltpu.SMEM)
    vmem = pl.BlockSpec(memory_space=pltpu.VMEM)
    dma = pltpu.SemaphoreType.DMA
    far_size = size // GROUP
    results = pl.pallas_call(
        functools.partial(kernel, size),
        out_shape=(
            jax.ShapeDtypeStruct((width, pixels), BF16),
            jax.ShapeDtypeStruct((width, pixels), BF16),
            jax.ShapeDtypeStruct(cheb_weight.shape, F32),
        ),
        in_specs=[hbm, vmem, hbm, vmem, smem, hbm, smem, smem, smem, smem, hbm],
        out_specs=(hbm, hbm, vmem),
        scratch_shapes=[
            pltpu.VMEM((width, pixels), BF16),
            pltpu.VMEM((width, pixels), BF16),
            pltpu.VMEM((blocks, nz, block, block), BF16),
            pltpu.VMEM((blocks, nz, block, block), BF16),
            pltpu.VMEM((1, rounds, hb, block, block), BF16),
            pltpu.VMEM((coups, block, block), BF16),
            *[pltpu.VMEM((blocks, width, block), BF16)] * 7,
            pltpu.VMEM((blocks, block, 2 * width), BF16),
            pltpu.VMEM((blocks + 1, width, block), F32),
            pltpu.VMEM((blocks + 1, width, block), F32),
            pltpu.VMEM((blocks + 1, width, block), F32),
            pltpu.VMEM((coups + 1, width, block), F32),
            pltpu.VMEM((coups + 1, width, block), F32),
            pltpu.VMEM((3, coups, width, block), BF16),
            pltpu.VMEM((3, coups, width, block), BF16),
            pltpu.VMEM((3, coups, width, block), BF16),
            pltpu.VMEM((3, coups, width, block), BF16),
            pltpu.VMEM((width, pixels), BF16),
            pltpu.VMEM((width, pixels), BF16),
            pltpu.VMEM((8, 128), I32),
            pltpu.SMEM((8, 128), I32),
            pltpu.SMEM((2, coups), I32),
            pltpu.SMEM((2, coups), I32),
            pltpu.VMEM((2 * width, 2 * width), F32),
            pltpu.VMEM((GROUP, 8, 2 * width), F32),
            pltpu.VMEM((8, 2 * width), F32),
            pltpu.VMEM((far_size, 8, 2 * width), F32),
            pltpu.VMEM((8, 2 * width), F32),
            pltpu.VMEM((GROUP, 8, 2 * width), F32),
            dma((3,)),
            dma((CHUNKS,)),
            dma,
            dma((2,)),
            dma((3,)),
            dma((3,)),
            dma((3,)),
            dma((3,)),
            dma,
            dma,
            dma,
            dma,
            dma,
            dma,
        ],
        compiler_params=pltpu.CompilerParams(
            collective_id=0, has_side_effects=True, vmem_limit_bytes=56 * 2**20
        ),
    )(features, cheb_weight, lap_tiles, col_index.T, col_index.T, cross_tiles, send_index.swapaxes(1, 2), row_index.swapaxes(1, 2), pair_on, blk_live, cotangent)
    return pl.pallas_call(
        handed_on,
        out_shape=tuple(jax.ShapeDtypeStruct(each.shape, each.dtype) for each in results),
        in_specs=[hbm] * 3,
        out_specs=(hbm,) * 3,
        scratch_shapes=[pltpu.VMEM(each.shape, each.dtype) for each in results] + [dma((3, PIECES)), dma((3, PIECES))],
    )(*results)


def solution(mesh):
    dom = P("dom")
    return jax.shard_map(
        functools.partial(local, mesh.shape["dom"]),
        mesh=mesh,
        in_specs=(P(None, "dom"), P(), dom, dom, dom, dom, dom, dom, dom, P(None, "dom")),
        out_specs=(P(None, "dom"), P(None, "dom"), P()),
        check_vma=False,
    )
```
